32 devices in a mesh: ka: 16 (over z, y, core), ga: 2 (over x).
Axes of the slice: x: 2, y: 2, z: 4, core: 2. Of those that a mesh axis runs over, the one named last changes fastest.
Arguments:
- pair_density: bfloat16 [64, 64, 1536], P('ka', None, 'ga'), may hold values from -0.15625 to 0.15625
- screened: bfloat16 [3, 1536, 1536], P(None, 'ga'), as said below
- vectors: bfloat16 [64, 64, 128], P('ka'), may hold values from -6 to 6
- energy: float32 [64, 64], P('ka'), may hold values from 1 to 3
- transfer_index: int32 [64, 5, 4], P('ka'), may hold values from 0 to 2, as said below
Outputs:
- image: float32 [64, 64, 128], P('ka')
The draws below stay inside these ranges and needn't reach their ends.
Inputs may be any that keep to these rules, and one draw needn't show every extreme that they name: `transfer_index`: every value from 0 to 2 may occur; both ends occur; the entry for the pair (k, k2) equals the entry for the pair (k2, k). `screened`: each slice is a symmetric matrix.
All inputs are finite; a program needn't handle non-finite values.
Results may differ from the reference program's by a relative error of at most 0.0019.
Values may be sent and summed in bfloat16 or wider, within the bound.
A program may use at most 64 MiB of HBM per device.

```python
import math
import jax
import jax.numpy as jnp
from jax import lax

NV = 8
NC = 8
NG = 1536
K_DEV = 4
NQ = 3
NB = 128
NK = 64
N_KA = 16


def draw_screened(key, part):
    key = jax.random.fold_in(key, 11)
    first, second = jax.random.split(key, 2)
    base = jax.random.normal(first, (NQ, NG, NG))
    diagonal = jnp.exp(jax.random.uniform(second, (NQ, NG), minval=math.log(0.5), maxval=math.log(4.0)))
    spread = (base + jnp.swapaxes(base, 1, 2)) * (1.5 / math.sqrt(2.0 * NG))
    identity = (lax.broadcasted_iota(jnp.int32, (NG, NG), 0) == lax.broadcasted_iota(jnp.int32, (NG, NG), 1)).astype(jnp.float32)
    return (spread + diagonal[:, :, None] * identity).astype(jnp.bfloat16)


def draw_transfer_index(key, part):
    key = jax.random.fold_in(key, 5)
    table = jax.random.randint(key, (NK, NK), 0, NQ)
    lower = lax.broadcasted_iota(jnp.int32, (NK, NK), 0) <= lax.broadcasted_iota(jnp.int32, (NK, NK), 1)
    table = jnp.where(lower, table, table.T)
    table = table.at[0, 1].set(0).at[1, 0].set(0).at[0, 0].set(NQ - 1)
    blocks = NK // K_DEV
    points = lax.broadcasted_iota(jnp.int32, (NK, 5, K_DEV), 0)
    offsets = lax.broadcasted_iota(jnp.int32, (NK, 5, K_DEV), 1)
    slots = lax.broadcasted_iota(jnp.int32, (NK, 5, K_DEV), 2)
    partner = (points // K_DEV + offsets - 2) % blocks * K_DEV + slots
    return table[points, partner].astype(jnp.int32)


def levels(own_key, dims, pieces, least, high):
    gain = 1.0
    for axis_at, parts in pieces:
        steps = jax.random.uniform(jax.random.fold_in(jax.random.fold_in(own_key, 6), axis_at), (parts,), jnp.float32, least / len(pieces), high / len(pieces))
        gain = gain * jnp.repeat(jnp.exp(steps), dims[axis_at] // parts).reshape((-1,) + (1,) * (len(dims) - 1 - axis_at))
    return gain


def scatter_about(rng, extent, scale, most, shards=(), held_as=jnp.bfloat16):
    level = levels(rng, extent, shards, -0.22, 0.18) if shards else 1.0
    drawn = jax.random.normal(rng, extent, jnp.float32) * scale * level
    return jnp.minimum(jnp.maximum(drawn, -most), most).astype(held_as)


def setup_inputs(seed: int = 0) -> dict:
    key_list = jax.random.split(jax.random.key(seed), 6)
    pair_density = scatter_about(key_list[0], (NK, NV * NC, NG), NG ** -0.5, 0.15625, ((0, 16), (2, 2)))
    screened = draw_screened(jax.random.fold_in(key_list[5], 71), 0)
    vectors = scatter_about(key_list[2], (NK, NV * NC, NB), 1.0, 6.0, ((0, 16),))
    energy = jnp.clip(1.0 + 2.0 * jax.random.uniform(key_list[3], (NK, NV * NC), jnp.float32) ** levels(key_list[3], (NK, NV * NC), ((0, 16),), -0.2, 0.2), 1.0, 3.0)
    transfer_index = draw_transfer_index(jax.random.fold_in(key_list[5], 71), 0)
    return dict(pair_density=pair_density, screened=screened, vectors=vectors, energy=energy, transfer_index=transfer_index)


def reference(pair_density, screened, vectors, energy, transfer_index):
    screening = screened.astype(jnp.float32)
    per_block = pair_density.shape[0] // N_KA
    by_block = pair_density.reshape(N_KA, per_block, pair_density.shape[1], pair_density.shape[2])
    vec_block = vectors.astype(jnp.float32).reshape(N_KA, per_block, vectors.shape[1], vectors.shape[2])
    idx_block = transfer_index.reshape(N_KA, per_block, 5, per_block)
    partners = jnp.arange(per_block, dtype=jnp.int32)

    def right_block(block_index):
        dens = by_block[block_index].astype(jnp.float32)
        product = jnp.einsum('qgh,jth->jqgt', screening, dens, precision=lax.Precision.HIGHEST)
        return product.astype(jnp.bfloat16)

    right_all = lax.map(right_block, jnp.arange(N_KA, dtype=jnp.int32))

    def one_block(block_index):
        own = by_block[block_index].astype(jnp.float32)
        running = jnp.zeros((per_block, vectors.shape[1], vectors.shape[2]), jnp.float32)
        for offset in range(5):
            other = (block_index + offset - 2) % N_KA
            picks = idx_block[block_index][:, offset, :].astype(jnp.int32)
            chosen = right_all[other][partners[None, :], picks].astype(jnp.float32)
            blocks = jnp.einsum('ksg,kjgt->kjst', own, chosen, precision=lax.Precision.HIGHEST)
            running = running + jnp.einsum('kjst,jtb->ksb', blocks, vec_block[other], precision=lax.Precision.HIGHEST)
        return running

    coupled = lax.map(one_block, jnp.arange(N_KA, dtype=jnp.int32))
    return energy[:, :, None] * vectors.astype(jnp.float32) + coupled.reshape(vectors.shape)
```

```python
import functools

import jax
import jax.numpy as jnp
from jax import lax
from jax.experimental import pallas as pl
from jax.experimental.pallas import tpu as pltpu
from jax.sharding import PartitionSpec as P

MESH = pl.DeviceIdType.MESH
NT = (((1,), (1,)), ((), ()))
TN = (((0,), (0,)), ((), ()))
PIECES = 3


def shifted(value, axis, by):
    length = lax.axis_size(axis)
    return lax.ppermute(value, axis, [(i, (i + by) % length) for i in range(length)])


def general(pair_density, screened, vectors, energy, transfer_index):
    count = screened.shape[0]
    gathered = lax.all_gather(pair_density, "ga", axis=2, tiled=True)
    own = jnp.einsum(
        "qgh,ksh->kqsg", screened, gathered, preferred_element_type=jnp.float32
    ).astype(jnp.bfloat16)
    coupled = 0.0
    for distance in (0, 1, -1, 2, -2):
        dens, vecs = pair_density, vectors
        if distance:
            dens, vecs = shifted((dens, vecs), "ka", distance)
        every = jnp.einsum("kqsg,jtg->kqsjt", own, dens, preferred_element_type=jnp.float32)
        picks = transfer_index[:, 2 - distance, :][:, None, :, None]
        blocks = every[:, 0]
        for q in range(1, count):
            blocks = jnp.where(picks == q, every[:, q], blocks)
        coupled = coupled + jnp.einsum(
            "ksjt,jtb->ksb", blocks, vecs.astype(jnp.float32), precision=lax.Precision.HIGHEST
        )
    summed = lax.psum(coupled, "ga")
    return energy[:, :, None] * vectors.astype(jnp.float32) + summed


def pair_kernel(
    n, nq, k_dev, states,
    x_hbm, v_hbm, idx_hbm, e_hbm, w_hbm, out,
    x, v, idx, e, wv, xo, x2, v2, x3, v3, racc, r, c1s, c1r, c2s, c2r, ts, tr,
    wsem, gs, gr, ss, sr,
):
    me = lax.axis_index("ka")
    gx = lax.axis_index("ga")
    odd = lax.rem(me, 2)
    rows, gl = x.shape
    small = [
        pltpu.make_async_copy(src, dst, wsem.at[nq + i])
        for i, (src, dst) in enumerate(((x_hbm, x), (v_hbm, v), (idx_hbm, idx), (e_hbm, e)))
    ]
    for load in small:
        load.start()

    def at(by):
        return lax.rem(me + by + n, n)

    def to(ka, ga=gx):
        return {"ka": ka, "ga": ga}

    def remote(src, dst, s, where):
        return pltpu.make_async_remote_copy(
            src_ref=src, dst_ref=dst, send_sem=ss.at[s], recv_sem=sr.at[s],
            device_id=where, device_id_type=MESH,
        )

    loads = [pltpu.make_async_copy(w_hbm.at[q], wv.at[q], wsem.at[q]) for q in range(nq)]
    for load in loads:
        load.start()

    barrier = pltpu.get_barrier_semaphore()
    for by in (-2, -1, 1, 2):
        pl.semaphore_signal(barrier, inc=1, device_id=to(at(by)), device_id_type=MESH)
    pl.semaphore_signal(barrier, inc=1, device_id=to(me, 1 - gx), device_id_type=MESH)
    pl.semaphore_wait(barrier, 5)

    piece = gl // PIECES
    gathers = []
    for c in range(PIECES):
        cols = pl.ds(c * piece, piece)
        gathers.append(
            pltpu.make_async_remote_copy(
                src_ref=x_hbm.at[:, cols], dst_ref=xo.at[:, cols],
                send_sem=gs.at[c], recv_sem=gr.at[c],
                device_id=to(me, 1 - gx), device_id_type=MESH,
            )
        )
    across = to(at(4 * odd - 2))
    core = to(at(1 - 2 * odd))

    def parts(src, dst, first, where):
        return [
            remote(
                src.at[:, pl.ds(c * piece, piece)], dst.at[:, pl.ds(c * piece, piece)],
                first + c, where,
            )
            for c in range(PIECES)
        ]

    far = parts(x_hbm, x2, 0, across)
    far_v = remote(v_hbm, v2, PIECES, across)
    near_odd = parts(x_hbm, x3, PIECES + 1, core)
    near_even = parts(x2, x3, PIECES + 1, core)
    near_odd_v = remote(v_hbm, v3, 2 * PIECES + 1, core)
    near_even_v = remote(v2, v3, 2 * PIECES + 1, core)
    last = 2 * PIECES + 2

    for c in range(PIECES):
        gathers[c].start()
        far[c].start()
    far_v.start()

    @pl.when(odd == 1)
    def _():
        for copy in near_odd + [near_odd_v]:
            copy.start()

    own_at = pl.multiple_of(gx * gl, 128)
    other_at = pl.multiple_of((1 - gx) * gl, 128)

    for load in small:
        load.wait()
    one = lax.broadcasted_iota(jnp.int32, (states, states), 0)
    one = one == lax.broadcasted_iota(jnp.int32, (states, states), 1)
    for k in range(k_dev):
        at_k = slice(k * states, (k + 1) * states)
        column = jnp.sum(jnp.where(one, e[k:k + 1, :], 0.0), axis=1, keepdims=True)
        out[at_k] = column * v[at_k].astype(jnp.float32)
    for q in range(nq):
        loads[q].wait()
        racc[q] = lax.dot_general(
            wv[q, :, pl.ds(own_at, gl)], x[...], NT, preferred_element_type=jnp.float32
        )

    for c in range(PIECES):
        gathers[c].wait_recv()
        cols = pl.ds(pl.multiple_of(other_at + c * piece, 128), piece)
        for q in range(nq):
            new = racc[q] + lax.dot_general(
                wv[q, :, cols], xo[:, c * piece:(c + 1) * piece], NT,
                preferred_element_type=jnp.float32,
            )
            if c < PIECES - 1:
                racc[q] = new
            else:
                r[q] = new.astype(jnp.bfloat16)
        far[c].wait_recv()

        @pl.when(odd == 0)
        def _(c=c):
            near_even[c].start()

    far_v.wait_recv()

    @pl.when(odd == 0)
    def _():
        near_even_v.start()

    lane = lax.broadcasted_iota(jnp.int32, (states, rows), 1) // states

    def kernel_of(dens, table):
        every = [
            jnp.dot(dens[...], r[q], preferred_element_type=jnp.float32) for q in range(nq)
        ]
        strips = []
        for j in range(k_dev):
            at_j = slice(j * states, (j + 1) * states)
            pick = jnp.zeros((states, rows), jnp.int32)
            for k in range(k_dev):
                pick = jnp.where(lane == k, table[k:k + 1, j:j + 1], pick)
            strip = every[0][at_j]
            for q in range(1, nq):
                strip = jnp.where(pick == q, every[q][at_j], strip)
            strips.append(strip)
        block = jnp.concatenate(strips, axis=0)
        high = block.astype(jnp.bfloat16)
        return high, (block - high.astype(jnp.float32)).astype(jnp.bfloat16)

    def forth(pair, vecs):
        return sum(jnp.dot(p, vecs[...], preferred_element_type=jnp.float32) for p in pair)

    def back(pair, vecs):
        return sum(
            lax.dot_general(p, vecs[...], TN, preferred_element_type=jnp.float32) for p in pair
        )

    pair1 = kernel_of(x2, jnp.where(odd == 1, idx[:, :, 0], idx[:, :, 4]))
    c1s[...] = forth(pair1, v).astype(jnp.bfloat16)
    back1 = remote(c1s, c1r, last, to(at(2 - 4 * odd)))
    back1.start()

    for copy in near_odd + [near_odd_v]:
        copy.wait_recv()
    pair2 = kernel_of(x3, idx[:, :, 3])
    c2s[...] = forth(pair2, v).astype(jnp.bfloat16)
    back2 = remote(c2s, c2r, last + 1, to(at(1)))
    back2.start()

    total = back(pair1, v2) + back(pair2, v3) + forth(kernel_of(x, idx[:, :, 2]), v)
    back1.wait_recv()
    back2.wait_recv()
    total += c1r[...].astype(jnp.float32) + c2r[...].astype(jnp.float32)
    ts[...] = total.astype(jnp.bfloat16)
    swap = remote(ts, tr, last + 2, to(me, 1 - gx))
    swap.start()
    for copy in gathers + far + near_odd + [far_v, near_odd_v, back1, back2]:
        copy.wait_send()
    swap.wait()
    out[...] += ts[...].astype(jnp.float32) + tr[...].astype(jnp.float32)


def local(pair_density, screened, vectors, energy, transfer_index):
    n = lax.axis_size("ka")
    k_dev, states, gl = pair_density.shape
    nq, _, ng = screened.shape
    width = vectors.shape[2]
    fits = gl % (128 * PIECES) == 0 and states % 16 == 0 and width % 128 == 0
    if lax.axis_size("ga") != 2 or n < 6 or n % 2 or not fits:
        return general(pair_density, screened, vectors, energy, transfer_index)
    rows = k_dev * states
    half = jnp.bfloat16
    hbm = pl.BlockSpec(memory_space=pl.ANY)
    image = pl.pallas_call(
        functools.partial(pair_kernel, n, nq, k_dev, states),
        out_shape=jax.ShapeDtypeStruct((rows, width), jnp.float32),
        in_specs=[hbm] * 5,
        out_specs=pl.BlockSpec(memory_space=pltpu.VMEM),
        scratch_shapes=[
            pltpu.VMEM((rows, gl), half),
            pltpu.VMEM((rows, width), half),
            pltpu.VMEM((k_dev, k_dev, 5), jnp.int32),
            pltpu.VMEM((k_dev, states), jnp.float32),
            pltpu.VMEM((nq, gl, ng), half),
            pltpu.VMEM((rows, gl), half),
            pltpu.VMEM((rows, gl), half),
            pltpu.VMEM((rows, width), half),
            pltpu.VMEM((rows, gl), half),
            pltpu.VMEM((rows, width), half),
            pltpu.VMEM((nq, gl, rows), jnp.float32),
            pltpu.VMEM((nq, gl, rows), half),
        ]
        + [pltpu.VMEM((rows, width), half)] * 6
        + [
            pltpu.SemaphoreType.DMA((nq + 4,)),
            pltpu.SemaphoreType.DMA((PIECES,)),
            pltpu.SemaphoreType.DMA((PIECES,)),
            pltpu.SemaphoreType.DMA((2 * PIECES + 5,)),
            pltpu.SemaphoreType.DMA((2 * PIECES + 5,)),
        ],
        compiler_params=pltpu.CompilerParams(
            collective_id=0, has_side_effects=True, vmem_limit_bytes=63 * 1024 * 1024 + 512 * 1024
        ),
        cost_estimate=pl.CostEstimate(
            flops=2 * nq * gl * rows * (ng + 3 * rows),
            bytes_accessed=2 * nq * gl * ng, transcendentals=0,
        ),
    )(
        pair_density.reshape(rows, gl), vectors.reshape(rows, width),
        jnp.swapaxes(transfer_index, 1, 2), energy, screened
    )
    return image.reshape(k_dev, states, width)


def solution(mesh):
    return jax.shard_map(
        local,
        mesh=mesh,
        in_specs=(
            P("ka", None, "ga"),
            P(None, "ga", None),
            P("ka", None, None),
            P("ka", None),
            P("ka", None, None),
        ),
        out_specs=P("ka", None, None),
        check_vma=False,
    )
```

```python
import functools

import jax
import jax.numpy as jnp
from jax import lax
from jax.experimental import pallas as pl
from jax.experimental.pallas import tpu as pltpu
from jax.sharding import PartitionSpec as P

MESH = pl.DeviceIdType.MESH
NT = (((1,), (1,)), ((), ()))
TN = (((0,), (0,)), ((), ()))
PIECES = 3


def shifted(value, axis, by):
    length = lax.axis_size(axis)
    return lax.ppermute(value, axis, [(i, (i + by) % length) for i in range(length)])


def general(pair_density, screened, vectors, energy, transfer_index):
    count = screened.shape[0]
    gathered = lax.all_gather(pair_density, "ga", axis=2, tiled=True)
    own = jnp.einsum(
        "qgh,ksh->kqsg", screened, gathered, preferred_element_type=jnp.float32
    ).astype(jnp.bfloat16)
    coupled = 0.0
    for distance in (0, 1, -1, 2, -2):
        dens, vecs = pair_density, vectors
        if distance:
            dens, vecs = shifted((dens, vecs), "ka", distance)
        every = jnp.einsum("kqsg,jtg->kqsjt", own, dens, preferred_element_type=jnp.float32)
        picks = transfer_index[:, 2 - distance, :][:, None, :, None]
        blocks = every[:, 0]
        for q in range(1, count):
            blocks = jnp.where(picks == q, every[:, q], blocks)
        coupled = coupled + jnp.einsum(
            "ksjt,jtb->ksb", blocks, vecs.astype(jnp.float32), precision=lax.Precision.HIGHEST
        )
    summed = lax.psum(coupled, "ga")
    return energy[:, :, None] * vectors.astype(jnp.float32) + summed


def pair_kernel(
    n, nq, k_dev, states,
    x_hbm, v_hbm, idx_hbm, e_hbm, w_hbm, out,
    x, v, idx, e, wv, xo, x2, v2, x3, v3, racc, r, c1s, c1r, c1x, c2s, c2r, c2x, ts, tr,
    wsem, gs, gr, ss, sr,
):
    me = lax.axis_index("ka")
    gx = lax.axis_index("ga")
    odd = lax.rem(me, 2)
    rows, gl = x.shape
    small = [
        pltpu.make_async_copy(src, dst, wsem.at[nq + i])
        for i, (src, dst) in enumerate(((x_hbm, x), (v_hbm, v), (idx_hbm, idx), (e_hbm, e)))
    ]
    for load in small:
        load.start()

    def at(by):
        return lax.rem(me + by + n, n)

    def to(ka, ga=gx):
        return {"ka": ka, "ga": ga}

    def remote(src, dst, s, where):
        return pltpu.make_async_remote_copy(
            src_ref=src, dst_ref=dst, send_sem=ss.at[s], recv_sem=sr.at[s],
            device_id=where, device_id_type=MESH,
        )

    loads = [pltpu.make_async_copy(w_hbm.at[q], wv.at[q], wsem.at[q]) for q in range(nq)]
    for load in loads:
        load.start()

    barrier = pltpu.get_barrier_semaphore()
    for by in (-2, -1, 1, 2):
        pl.semaphore_signal(barrier, inc=1, device_id=to(at(by)), device_id_type=MESH)
    for by in (-2, -1, 0, 1, 2):
        pl.semaphore_signal(barrier, inc=1, device_id=to(at(by), 1 - gx), device_id_type=MESH)
    pl.semaphore_wait(barrier, 9)

    piece = gl // PIECES
    gathers = []
    for c in range(PIECES):
        cols = pl.ds(c * piece, piece)
        gathers.append(
            pltpu.make_async_remote_copy(
                src_ref=x_hbm.at[:, cols], dst_ref=xo.at[:, cols],
                send_sem=gs.at[c], recv_sem=gr.at[c],
                device_id=to(me, 1 - gx), device_id_type=MESH,
            )
        )
    across = to(at(4 * odd - 2))
    core = to(at(1 - 2 * odd))

    def parts(src, dst, first, where):
        return [
            remote(
                src.at[:, pl.ds(c * piece, piece)], dst.at[:, pl.ds(c * piece, piece)],
                first + c, where,
            )
            for c in range(PIECES)
        ]

    far = parts(x_hbm, x2, 0, across)
    far_v = remote(v_hbm, v2, PIECES, across)
    near_odd = parts(x_hbm, x3, PIECES + 1, core)
    near_even = parts(x2, x3, PIECES + 1, core)
    near_odd_v = remote(v_hbm, v3, 2 * PIECES + 1, core)
    near_even_v = remote(v2, v3, 2 * PIECES + 1, core)
    last = 2 * PIECES + 2

    for c in range(PIECES):
        gathers[c].start()
        far[c].start()
    far_v.start()

    @pl.when(odd == 1)
    def _():
        for copy in near_odd + [near_odd_v]:
            copy.start()

    own_at = pl.multiple_of(gx * gl, 128)
    other_at = pl.multiple_of((1 - gx) * gl, 128)

    for load in small:
        load.wait()
    one = lax.broadcasted_iota(jnp.int32, (states, states), 0)
    one = one == lax.broadcasted_iota(jnp.int32, (states, states), 1)
    for k in range(k_dev):
        at_k = slice(k * states, (k + 1) * states)
        column = jnp.sum(jnp.where(one, e[k:k + 1, :], 0.0), axis=1, keepdims=True)
        out[at_k] = column * v[at_k].astype(jnp.float32)
    for q in range(nq):
        loads[q].wait()
        racc[q] = lax.dot_general(
            wv[q, :, pl.ds(own_at, gl)], x[...], NT, preferred_element_type=jnp.float32
        )

    for c in range(PIECES):
        gathers[c].wait_recv()
        cols = pl.ds(pl.multiple_of(other_at + c * piece, 128), piece)
        for q in range(nq):
            new = racc[q] + lax.dot_general(
                wv[q, :, cols], xo[:, c * piece:(c + 1) * piece], NT,
                preferred_element_type=jnp.float32,
            )
            if c < PIECES - 1:
                racc[q] = new
            else:
                r[q] = new.astype(jnp.bfloat16)
        far[c].wait_recv()

        @pl.when(odd == 0)
        def _(c=c):
            near_even[c].start()

    far_v.wait_recv()

    @pl.when(odd == 0)
    def _():
        near_even_v.start()

    lane = lax.broadcasted_iota(jnp.int32, (states, rows), 1) // states

    def kernel_of(dens, table):
        every = [
            jnp.dot(dens[...], r[q], preferred_element_type=jnp.float32) for q in range(nq)
        ]
        strips = []
        for j in range(k_dev):
            at_j = slice(j * states, (j + 1) * states)
            pick = jnp.zeros((states, rows), jnp.int32)
            for k in range(k_dev):
                pick = jnp.where(lane == k, table[k:k + 1, j:j + 1], pick)
            strip = every[0][at_j]
            for q in range(1, nq):
                strip = jnp.where(pick == q, every[q][at_j], strip)
            strips.append(strip)
        block = jnp.concatenate(strips, axis=0)
        high = block.astype(jnp.bfloat16)
        return high, (block - high.astype(jnp.float32)).astype(jnp.bfloat16)

    def forth(pair, vecs):
        return sum(jnp.dot(p, vecs[...], preferred_element_type=jnp.float32) for p in pair)

    def back(pair, vecs):
        return sum(
            lax.dot_general(p, vecs[...], TN, preferred_element_type=jnp.float32) for p in pair
        )

    pair1 = kernel_of(x2, jnp.where(odd == 1, idx[:, :, 0], idx[:, :, 4]))
    c1s[...] = forth(pair1, v).astype(jnp.bfloat16)
    back1 = remote(c1s, c1r, last, to(at(2 - 4 * odd)))
    back1.start()
    cross1 = remote(c1s, c1x, last + 4, to(at(2 - 4 * odd), 1 - gx))
    cross1.start()

    total = back(pair1, v2) + forth(kernel_of(x, idx[:, :, 2]), v)
    for copy in near_odd + [near_odd_v]:
        copy.wait_recv()
    pair2 = kernel_of(x3, idx[:, :, 3])
    c2s[...] = forth(pair2, v).astype(jnp.bfloat16)
    back2 = remote(c2s, c2r, last + 1, to(at(1)))
    back2.start()
    cross2 = remote(c2s, c2x, last + 3, to(at(1), 1 - gx))
    cross2.start()

    total += back(pair2, v3)
    ts[...] = total.astype(jnp.bfloat16)
    swap = remote(ts, tr, last + 2, to(me, 1 - gx))
    swap.start()
    for copy in gathers + far + near_odd + [far_v, near_odd_v, back1, back2, cross1, cross2]:
        copy.wait_send()
    back1.wait_recv()
    cross1.wait_recv()
    out[...] += c1r[...].astype(jnp.float32) + c1x[...].astype(jnp.float32)
    back2.wait_recv()
    cross2.wait_recv()
    out[...] += c2r[...].astype(jnp.float32) + c2x[...].astype(jnp.float32)
    swap.wait()
    out[...] += ts[...].astype(jnp.float32) + tr[...].astype(jnp.float32)


def local(pair_density, screened, vectors, energy, transfer_index):
    n = lax.axis_size("ka")
    k_dev, states, gl = pair_density.shape
    nq, _, ng = screened.shape
    width = vectors.shape[2]
    fits = gl % (128 * PIECES) == 0 and states % 16 == 0 and width % 128 == 0
    if lax.axis_size("ga") != 2 or n < 6 or n % 2 or not fits:
        return general(pair_density, screened, vectors, energy, transfer_index)
    rows = k_dev * states
    half = jnp.bfloat16
    hbm = pl.BlockSpec(memory_space=pl.ANY)
    image = pl.pallas_call(
        functools.partial(pair_kernel, n, nq, k_dev, states),
        out_shape=jax.ShapeDtypeStruct((rows, width), jnp.float32),
        in_specs=[hbm] * 5,
        out_specs=pl.BlockSpec(memory_space=pltpu.VMEM),
        scratch_shapes=[
            pltpu.VMEM((rows, gl), half),
            pltpu.VMEM((rows, width), half),
            pltpu.VMEM((k_dev, k_dev, 5), jnp.int32),
            pltpu.VMEM((k_dev, states), jnp.float32),
            pltpu.VMEM((nq, gl, ng), half),
            pltpu.VMEM((rows, gl), half),
            pltpu.VMEM((rows, gl), half),
            pltpu.VMEM((rows, width), half),
            pltpu.VMEM((rows, gl), half),
            pltpu.VMEM((rows, width), half),
            pltpu.VMEM((nq, gl, rows), jnp.float32),
            pltpu.VMEM((nq, gl, rows), half),
        ]
        + [pltpu.VMEM((rows, width), half)] * 8
        + [
            pltpu.SemaphoreType.DMA((nq + 4,)),
            pltpu.SemaphoreType.DMA((PIECES,)),
            pltpu.SemaphoreType.DMA((PIECES,)),
            pltpu.SemaphoreType.DMA((2 * PIECES + 7,)),
            pltpu.SemaphoreType.DMA((2 * PIECES + 7,)),
        ],
        compiler_params=pltpu.CompilerParams(
            collective_id=0, has_side_effects=True, vmem_limit_bytes=63 * 1024 * 1024 + 512 * 1024
        ),
        cost_estimate=pl.CostEstimate(
            flops=2 * nq * gl * rows * (ng + 3 * rows),
            bytes_accessed=2 * nq * gl * ng, transcendentals=0,
        ),
    )(
        pair_density.reshape(rows, gl), vectors.reshape(rows, width),
        jnp.swapaxes(transfer_index, 1, 2), energy, screened
    )
    return image.reshape(k_dev, states, width)


def solution(mesh):
    return jax.shard_map(
        local,
        mesh=mesh,
        in_specs=(
            P("ka", None, "ga"),
            P(None, "ga", None),
            P("ka", None, None),
            P("ka", None),
            P("ka", None, None),
        ),
        out_specs=P("ka", None, None),
        check_vma=False,
    )
```
